768 devices in a mesh: fsdp: 96 (over z_lo, x, y), dp: 8 (over z_hi, core).
Axes of the slice: x: 4, y: 8, z: 12 (z_hi: 4, z_lo: 3; z = z_hi * 3 + z_lo), core: 2. Of those that a mesh axis runs over, the one named last changes fastest.
Arguments:
- hidden: bfloat16 [98304, 8192], P(('fsdp', 'dp')), may hold values from -6 to 6
- norm_gain: float32 [8192], replicated, may hold values from 0.1 to 1.9
- proj: bfloat16 [768, 8192], P('fsdp'), may hold values from -2 to 2
- assign: int32 [96, 1024], P('fsdp'), may hold values from 0 to 1023, as said below
- lengths: int32 [8, 4], P('dp'), may hold values from 1 to 6144, 12288 in all within a row
Outputs:
- head_out: bfloat16 [98304, 512], P(('fsdp', 'dp'))
The draws below stay inside these ranges and needn't reach their ends.
Inputs may be any that keep to these rules, and one draw needn't show every extreme that they name: Each row assign[f] is a permutation of the 1024 indices; of the 128 home rows of one device (entries d * 128 to (d + 1) * 128 - 1), exactly 16 go to each data group g (values g * 128 to g * 128 + 127).
All inputs are finite; a program needn't handle non-finite values.
Results may differ from the reference program's by a relative error of at most 0.02.
The reference program's roundings to bfloat16 on the way count: a program that leaves them out, or rounds other values in their place, can miss the bound.
Values may be sent and summed in bfloat16 or wider, within the bound.
No kernel may reach another device: no remote copies, remote signals or barrier semaphores. Data moves between devices by JAX's collectives and lax.ppermute only.
A program may use at most 64 MiB of HBM per device.

```python
import math
import jax
import jax.numpy as jnp
import numpy as np
from jax import lax

D = 8192
HD = 128
QH = 4
ROWS = 128
SPAN = 48
LMAX = 6144
GROUP = 12288
NSEQ = 4
TOKENS = 98304
N_FSDP = 96
N_DP = 8


def draw_proj(key, part):
    key = jax.random.fold_in(key, 1)
    values = jax.random.normal(key, ((QH + 2) * HD, D), jnp.float32)
    return (values / math.sqrt(D)).astype(jnp.bfloat16)


def draw_assign(key, part):
    key = jax.random.fold_in(key, 2)
    per_peer = ROWS // N_DP

    def shuffled(shuffle_key, source):
        return jax.random.permutation(shuffle_key, source)

    def one_column(column_key):
        send_key, place_key = jax.random.split(column_key)
        source_groups = jnp.arange(ROWS, dtype=jnp.int32) // per_peer
        group_table = jax.vmap(shuffled, in_axes=(0, None))(jax.random.split(send_key, N_DP), source_groups)
        flat_groups = group_table.reshape(-1)
        one_hot = (flat_groups[:, None] == jnp.arange(N_DP, dtype=jnp.int32)[None, :]).astype(jnp.int32)
        ranking = jnp.sum((jnp.cumsum(one_hot, axis=0) - 1) * one_hot, axis=1)
        slot_table = jax.vmap(shuffled, in_axes=(0, None))(jax.random.split(place_key, N_DP), jnp.arange(ROWS, dtype=jnp.int32))
        chosen = slot_table[flat_groups, ranking]
        return (flat_groups * ROWS + chosen).astype(jnp.int32)
    return jax.vmap(one_column)(jax.random.split(key, N_FSDP))


def shard_levels(stream_key, extent, cuts, low, high):
    level, own = 1.0, jax.random.fold_in(stream_key, 6)
    for axis_at, shards_of in cuts:
        heights = jnp.exp(jax.random.uniform(jax.random.fold_in(own, axis_at), (shards_of,), jnp.float32, low / len(cuts), high / len(cuts)))
        level = level * jnp.repeat(heights, extent[axis_at] // shards_of).reshape([-1 if axis == axis_at else 1 for axis in range(len(extent))])
    return level


def length_profile(amount, total, bound, skew):
    portions = [(1 << 20) // math.isqrt(rank ** skew) + 1 for rank in range(2, amount + 1)]
    rest, counts = total - bound - (amount - 1), [1] * (amount - 1)
    while rest > 0:
        free = [i for i in range(amount - 1) if counts[i] < bound]
        mass, remaining = sum([portions[i] for i in free]), rest
        for i in free:
            extra = min(bound - counts[i], max(1, remaining * portions[i] // mass), rest)
            counts[i] = counts[i] + extra
            rest = rest - extra
    return np.array([bound] + counts)


def uneven_parts(own_key, number_of, total, most, lean):
    if number_of == 2:
        one = jax.random.randint(own_key, (), max(1, total - most), min(most, total - 1) + 1)
        return jnp.stack([one, total - one])
    tallies = jnp.asarray(length_profile(number_of, total, most, lean), jnp.int32)
    twos = (number_of - 1) // 2
    giver, sink = tallies[1:1 + 2 * twos:2], tallies[2:2 + 2 * twos:2]
    slack = jnp.minimum(giver - 1, most - sink)
    shifted = jax.random.randint(jax.random.fold_in(own_key, 1), (twos,), 0, 1 << 20) % (slack + 1)
    tallies = tallies.at[1:1 + 2 * twos:2].set(giver - shifted).at[2:2 + 2 * twos:2].set(sink + shifted)
    return tallies[jax.random.permutation(jax.random.fold_in(own_key, 2), number_of)]


def scatter_about(rng, extent, scale, bound, shards=(), kind=jnp.bfloat16):
    factor_of = shard_levels(rng, extent, shards, -0.22, 0.18) if shards else 1.0
    values = jax.random.normal(rng, extent, jnp.float32) * scale * factor_of
    return jnp.minimum(jnp.maximum(values, -bound), bound).astype(kind)


def setup_inputs(seed: int = 0) -> dict:
    key_of = jax.random.split(jax.random.key(seed), 6)
    return {
        "hidden": scatter_about(key_of[0], (TOKENS, D), 1.0, 6.0, ((0, 768),)),
        "norm_gain": jnp.clip(1.0 + 0.18 * jax.random.normal(key_of[1], (D,), jnp.float32), 0.1, 1.9),
        "proj": draw_proj(jax.random.fold_in(key_of[5], 71), 0),
        "assign": draw_assign(jax.random.fold_in(key_of[5], 71), 0),
        "lengths": jax.vmap(lambda own: uneven_parts(own, NSEQ, GROUP, LMAX, 2))(jax.random.split(key_of[4], N_DP)).reshape((N_DP, NSEQ)).astype(jnp.int32),
    }


THETA = 1000000.0
EPSILON = 1e-06

def rms_normed(block_rows, norm_gain):
    widened = block_rows.astype(jnp.float32)
    inverse = lax.rsqrt(lax.optimization_barrier(jnp.mean(widened * widened, axis=1, keepdims=True)) + EPSILON)
    return (widened * inverse * norm_gain).astype(jnp.bfloat16)

def rotated(values, positions):
    half_width = values.shape[1] // 2
    inverse_freq = THETA ** (-(jnp.arange(half_width, dtype=jnp.float32) * 2.0) / values.shape[1])
    angles = positions.astype(jnp.float32)[:, None] * inverse_freq[None, :]
    cosine = jnp.cos(angles)
    sine_part = jnp.sin(angles)
    first_half = values[:, :half_width]
    second_half = values[:, half_width:]
    return jnp.concatenate([first_half * cosine - second_half * sine_part, second_half * cosine + first_half * sine_part], axis=1)

def segment_info(indices, seq_lengths):
    ends_at = jnp.cumsum(seq_lengths).astype(jnp.int32)
    finished = ends_at[None, :] <= indices[:, None]
    segment = lax.optimization_barrier(jnp.sum(finished.astype(jnp.int32), axis=1)).astype(jnp.int32)
    offset = lax.optimization_barrier(jnp.sum(jnp.where(finished, seq_lengths[None, :], 0), axis=1)).astype(jnp.int32)
    return (segment, (indices - offset).astype(jnp.int32))

def attend(queries, keypair, query_index, key_index, seq_lengths):
    head_dim = keypair.shape[1] // 2
    row_total = queries.shape[0]
    heads = queries.shape[1] // head_dim
    query_seg = segment_info(query_index, seq_lengths)[0]
    key_seg = segment_info(key_index, seq_lengths)[0]
    allowed = (key_seg[None, :] == query_seg[:, None]) & (key_index[None, :] <= query_index[:, None]) & (key_index[None, :] >= 0)
    key_part = keypair[:, :head_dim]
    value_part = keypair[:, head_dim:]

    def one_head(query_rows):
        scores = jnp.dot(query_rows, key_part.T, preferred_element_type=jnp.float32) / math.sqrt(head_dim)
        masked = jnp.where(allowed, scores, -jnp.inf)
        largest = lax.optimization_barrier(jnp.max(masked, axis=1, keepdims=True))
        powered = jnp.where(allowed, jnp.exp(masked - largest), 0.0)
        weights = (powered / lax.optimization_barrier(jnp.sum(powered, axis=1, keepdims=True))).astype(jnp.bfloat16)
        return jnp.dot(weights, value_part, preferred_element_type=jnp.float32).astype(jnp.bfloat16)
    head_major = queries.reshape(row_total, heads, head_dim).transpose(1, 0, 2)
    per_head = lax.map(one_head, head_major)
    return per_head.transpose(1, 0, 2).reshape(row_total, heads * head_dim)

def rotate_queries(query_cols, positions, heads):
    row_total = query_cols.shape[0]
    head_dim = query_cols.shape[1] // heads
    flat = query_cols.astype(jnp.float32).reshape(row_total * heads, head_dim)
    spun = rotated(flat, jnp.repeat(positions, heads))
    return spun.astype(jnp.bfloat16).reshape(row_total, heads * head_dim)

def reference(hidden, norm_gain, proj, assign, lengths):
    blocks = hidden.reshape(N_FSDP * N_DP, ROWS, D)
    width = (QH + 2) * HD

    def project_block(block_rows):
        normed = rms_normed(block_rows, norm_gain)
        return jnp.dot(normed, proj.T, preferred_element_type=jnp.float32).astype(jnp.bfloat16)
    projected = lax.map(project_block, blocks).reshape(N_FSDP, N_DP * ROWS, width)
    column_ids = jnp.arange(N_FSDP, dtype=jnp.int32)[:, None]
    placed = jnp.zeros_like(projected).at[column_ids, assign].set(projected)
    streams = placed.reshape(N_FSDP, N_DP, ROWS, width).transpose(1, 0, 2, 3).reshape(N_DP, GROUP, width)

    def one_group(packed):
        stream_rows, seq_lengths = packed
        stream_index = jnp.arange(GROUP, dtype=jnp.int32)
        positions = segment_info(stream_index, seq_lengths)[1]
        queries = rotate_queries(stream_rows[:, :QH * HD], positions, QH)
        keys_rot = rotated(stream_rows[:, QH * HD:(QH + 1) * HD].astype(jnp.float32), positions).astype(jnp.bfloat16)
        keypair = jnp.concatenate([keys_rot, stream_rows[:, (QH + 1) * HD:]], axis=1)
        padded = jnp.concatenate([jnp.zeros((SPAN * ROWS, 2 * HD), jnp.bfloat16), keypair], axis=0)

        def one_block(block_id):
            start = (block_id * ROWS).astype(jnp.int32)
            query_block = lax.dynamic_slice_in_dim(queries, start, ROWS, 0)
            key_block = lax.dynamic_slice_in_dim(padded, start, (SPAN + 1) * ROWS, 0)
            query_index = start + jnp.arange(ROWS, dtype=jnp.int32)
            key_index = start - SPAN * ROWS + jnp.arange((SPAN + 1) * ROWS, dtype=jnp.int32)
            return attend(query_block, key_block, query_index, key_index, seq_lengths)
        return lax.map(one_block, jnp.arange(N_FSDP, dtype=jnp.int32)).reshape(GROUP, QH * HD)
    attended = lax.map(one_group, (streams, lengths))
    out_columns = attended.reshape(N_DP, N_FSDP, ROWS, QH * HD).transpose(1, 0, 2, 3).reshape(N_FSDP, N_DP * ROWS, QH * HD)
    home_rows = jnp.take_along_axis(out_columns, assign[:, :, None], axis=1)
    return home_rows.reshape(TOKENS, QH * HD)
```

```python
import math

import jax
import jax.numpy as jnp
from jax import lax
from jax.sharding import Mesh, PartitionSpec as P

QH = 4
FSDP = ("zl", "x", "y")
DP = ("zh", "core")
SIZES = {"zl": 3, "x": 4, "y": 8, "zh": 4, "core": 2}

THETA = 1000000.0
EPSILON = 1e-06


def from_behind(value, axis, by):
    peers = lax.axis_size(axis)
    pairs = [(i, i + by) for i in range(peers) if 0 <= i + by < peers]
    return lax.ppermute(value, axis, pairs)


def rms_normed(block_rows, norm_gain):
    widened = block_rows.astype(jnp.float32)
    inverse = lax.rsqrt(jnp.mean(widened * widened, axis=1, keepdims=True) + EPSILON)
    return (widened * inverse * norm_gain).astype(jnp.bfloat16)


def rotated(values, positions):
    half_width = values.shape[1] // 2
    inverse_freq = THETA ** (-(jnp.arange(half_width, dtype=jnp.float32) * 2.0) / values.shape[1])
    angles = positions.astype(jnp.float32)[:, None] * inverse_freq[None, :]
    cosine = jnp.cos(angles)
    sine_part = jnp.sin(angles)
    first_half = values[:, :half_width]
    second_half = values[:, half_width:]
    return jnp.concatenate(
        [
            first_half * cosine - second_half * sine_part,
            second_half * cosine + first_half * sine_part,
        ],
        axis=1,
    )


def segment_info(indices, seq_lengths):
    ends_at = jnp.cumsum(seq_lengths)
    finished = ends_at[None, :] <= indices[:, None]
    segment = jnp.sum(finished.astype(jnp.int32), axis=1)
    offset = jnp.sum(jnp.where(finished, seq_lengths[None, :], 0), axis=1)
    return (segment, indices - offset)


def attend(queries, keypair, query_index, key_index, seq_lengths):
    head_dim = keypair.shape[1] // 2
    row_total = queries.shape[0]
    heads = queries.shape[1] // head_dim
    query_seg = segment_info(query_index, seq_lengths)[0]
    key_seg = segment_info(key_index, seq_lengths)[0]
    allowed = (
        (key_seg[None, :] == query_seg[:, None])
        & (key_index[None, :] <= query_index[:, None])
        & (key_index[None, :] >= 0)
    )
    key_part = keypair[:, :head_dim]
    value_part = keypair[:, head_dim:]

    def one_head(query_rows):
        scores = jnp.dot(query_rows, key_part.T, preferred_element_type=jnp.float32) / math.sqrt(
            head_dim
        )
        masked = jnp.where(allowed, scores, -jnp.inf)
        largest = jnp.max(masked, axis=1, keepdims=True)
        powered = jnp.where(allowed, jnp.exp(masked - largest), 0.0)
        weights = (powered / jnp.sum(powered, axis=1, keepdims=True)).astype(jnp.bfloat16)
        return jnp.dot(weights, value_part, preferred_element_type=jnp.float32).astype(jnp.bfloat16)

    head_major = queries.reshape(row_total, heads, head_dim).transpose(1, 0, 2)
    per_head = lax.map(one_head, head_major)
    return per_head.transpose(1, 0, 2).reshape(row_total, heads * head_dim)


def rotate_queries(query_cols, positions, heads):
    row_total = query_cols.shape[0]
    head_dim = query_cols.shape[1] // heads
    flat = query_cols.astype(jnp.float32).reshape(row_total * heads, head_dim)
    spun = rotated(flat, jnp.repeat(positions, heads))
    return spun.astype(jnp.bfloat16).reshape(row_total, heads * head_dim)


def z_shift(value, by):
    zl_size, zh_size = SIZES["zl"], SIZES["zh"]
    ring = zl_size * zh_size
    pairs = []
    for zl in range(zl_size):
        for zh in range(zh_size):
            to = (zh * zl_size + zl + by) % ring
            pairs.append((zl * zh_size + zh, (to % zl_size) * zh_size + to // zl_size))
    return lax.ppermute(value, ("zl", "zh"), pairs)


def by_class(own, before, after):
    zl = lax.axis_index("zl")
    stacked = jnp.stack([own, after, before])
    return jnp.stack(
        [
            lax.dynamic_index_in_dim(stacked, lax.rem(p - zl + 3, 3), 0, keepdims=False)
            for p in range(3)
        ]
    )


def spread_x(block):
    sent = jnp.broadcast_to(block[None], (SIZES["x"],) + block.shape)
    return lax.all_to_all(sent, "x", 0, 0, tiled=True)


def swap_core(value):
    return lax.ppermute(value, "core", [(0, 1), (1, 0)])


def project_home(normed, proj):
    rows, width = normed.shape
    core = lax.axis_index("core")
    half = width // 2
    mine = lax.dynamic_slice_in_dim(normed, core * half, half, 1)
    theirs = swap_core(lax.dynamic_slice_in_dim(normed, (1 - core) * half, half, 1))
    both = jnp.concatenate([mine, theirs], axis=0)
    shard = lax.dynamic_slice_in_dim(proj, core * half, half, 1)
    gathered = lax.all_gather(shard, "y", axis=0, tiled=True)
    cut = (half // 128 * 7 // 16) * 128
    one = gathered[:, :cut]
    one = by_class(one, z_shift(one, 1), z_shift(one, -1))
    one = spread_x(one).transpose(1, 0, 2, 3).reshape(-1, cut)
    two = spread_x(gathered[:, cut:]).reshape(-1, half - cut)
    two_before, two_after = z_shift(two, 1), z_shift(two, -1)

    def times(a, w):
        return lax.dot_general(a, w, (((1,), (1,)), ((), ())), preferred_element_type=jnp.float32)

    sum_one = times(both[:, :cut], one)
    rest = both[:, cut:]
    sum_two = by_class(times(rest, two), times(rest, two_before), times(rest, two_after))
    plane = sum_two.shape[2]
    total = jnp.concatenate(
        [sum_two[p] + sum_one[:, p * plane : (p + 1) * plane] for p in range(3)], axis=1
    )
    return (total[:rows] + swap_core(total[rows:])).astype(jnp.bfloat16)


def per_device(hidden, norm_gain, proj, assign, lengths):
    row_count = hidden.shape[0]
    groups = lax.axis_size(DP)
    per_peer = row_count // groups
    my_group = lax.axis_index(DP)
    column = assign[0]
    group_of = (column // row_count).reshape(groups, row_count)
    slot_of = (column % row_count).reshape(groups, row_count)
    group_ids = jnp.arange(groups, dtype=jnp.int32)
    one_hot = (group_of[:, :, None] == group_ids[None, None, :]).astype(jnp.int32)
    ranking = jnp.sum((jnp.cumsum(one_hot, axis=1) - 1) * one_hot, axis=2)
    buffer_pos = group_of * per_peer + ranking
    own_slots = lax.dynamic_index_in_dim(buffer_pos, my_group, 0, keepdims=False)
    send_index = (
        jnp.zeros((row_count,), jnp.int32).at[own_slots].set(jnp.arange(row_count, dtype=jnp.int32))
    )
    arrival = group_ids[:, None] * per_peer + ranking
    inbound = jnp.where(group_of == my_group, slot_of, row_count)
    place_index = (
        jnp.zeros((row_count,), jnp.int32)
        .at[inbound.reshape(-1)]
        .set(arrival.reshape(-1), mode="drop")
    )
    outbound = jnp.where(group_of == my_group, arrival, row_count)
    return_index = (
        jnp.zeros((row_count,), jnp.int32)
        .at[outbound.reshape(-1)]
        .set(slot_of.reshape(-1), mode="drop")
    )
    home = project_home(rms_normed(hidden, norm_gain), proj)
    outgoing = home[send_index].reshape(groups, per_peer, home.shape[1])
    arrived = lax.all_to_all(outgoing, DP, split_axis=0, concat_axis=0, tiled=True)
    projected = arrived.reshape(row_count, home.shape[1])[place_index]
    head_dim = projected.shape[1] // (QH + 2)
    seq_lengths = lengths[0]
    stream = lax.axis_index(FSDP) * row_count + jnp.arange(row_count, dtype=jnp.int32)
    positions = segment_info(stream, seq_lengths)[1]
    queries = rotate_queries(projected[:, : QH * head_dim], positions, QH)
    keys_rot = rotated(
        projected[:, QH * head_dim : (QH + 1) * head_dim].astype(jnp.float32), positions
    ).astype(jnp.bfloat16)
    keypair = jnp.concatenate([keys_rot, projected[:, (QH + 1) * head_dim :]], axis=1)
    reach_count = lax.axis_size(FSDP) // 2
    levels = reach_count.bit_length()
    window = keypair
    window_index = stream
    for level in range(levels):
        distance = 1 << level
        earlier = from_behind(window, FSDP, distance)
        window = jnp.concatenate([earlier, window], axis=0)
        window_index = jnp.concatenate([window_index - distance * row_count, window_index], axis=0)
    keep_rows = (reach_count + 1) * row_count
    window = window[window.shape[0] - keep_rows :]
    window_index = window_index[window_index.shape[0] - keep_rows :]
    attended = attend(queries, window, stream, window_index, seq_lengths)
    outgoing_back = attended[return_index].reshape(groups, per_peer, attended.shape[1])
    returned = lax.all_to_all(outgoing_back, DP, split_axis=0, concat_axis=0, tiled=True)
    return returned.reshape(row_count, attended.shape[1])[own_slots]


def solution(mesh):
    shape = [SIZES[name] for name in FSDP + DP]
    fine = Mesh(mesh.devices.reshape(shape), FSDP + DP)
    in_specs = (P(FSDP + DP, None), P(), P(FSDP, None), P(FSDP, None), P(DP, None))
    return jax.shard_map(
        per_device, mesh=fine, in_specs=in_specs, out_specs=P(FSDP + DP, None), check_vma=False
    )
```

```python
import functools
import math

import jax
import jax.numpy as jnp
from jax import lax
from jax.experimental import pallas as pl
from jax.experimental.pallas import tpu as pltpu
from jax.sharding import Mesh, PartitionSpec as P

QH = 4
FSDP = ("zl", "x", "y")
DP = ("zh", "core")
SIZES = {"zl": 3, "x": 4, "y": 8, "zh": 4, "core": 2}

THETA = 1000000.0
EPSILON = 1e-06


def rms_normed(block_rows, norm_gain):
    widened = block_rows.astype(jnp.float32)
    inverse = lax.rsqrt(jnp.mean(widened * widened, axis=1, keepdims=True) + EPSILON)
    return (widened * inverse * norm_gain).astype(jnp.bfloat16)


def rope_tables(positions, width):
    half_width = width // 2
    inverse_freq = THETA ** (-(jnp.arange(half_width, dtype=jnp.float32) * 2.0) / width)
    angles = positions.astype(jnp.float32)[:, None] * inverse_freq[None, :]
    cosine, sine = jnp.cos(angles), jnp.sin(angles)
    return jnp.concatenate([cosine, cosine], axis=1), jnp.concatenate([-sine, sine], axis=1)


def segment_info(indices, seq_lengths):
    ends_at = jnp.cumsum(seq_lengths)
    finished = ends_at[None, :] <= indices[:, None]
    segment = jnp.sum(finished.astype(jnp.int32), axis=1)
    offset = jnp.sum(jnp.where(finished, seq_lengths[None, :], 0), axis=1)
    return (segment, indices - offset, offset)


def z_shift(value, by):
    zl_size, zh_size = SIZES["zl"], SIZES["zh"]
    ring = zl_size * zh_size
    pairs = []
    for zl in range(zl_size):
        for zh in range(zh_size):
            to = (zh * zl_size + zl + by) % ring
            pairs.append((zl * zh_size + zh, (to % zl_size) * zh_size + to // zl_size))
    return lax.ppermute(value, ("zl", "zh"), pairs)


def spread(block, axis):
    sent = jnp.broadcast_to(block[None], (SIZES[axis],) + block.shape)
    return lax.all_to_all(sent, axis, 0, 0, tiled=True)


def swap_core(value):
    return lax.ppermute(value, "core", [(0, 1), (1, 0)])


def kernel_call(body, outs, scalars, flops, operands):
    spaces = [pltpu.SMEM] * scalars + [pltpu.VMEM] * (len(operands) - scalars)
    moved = sum(a.size * a.dtype.itemsize for a in list(operands) + list(outs))
    return pl.pallas_call(
        body,
        out_shape=outs,
        in_specs=[pl.BlockSpec(memory_space=space) for space in spaces],
        out_specs=[pl.BlockSpec(memory_space=pltpu.VMEM)] * len(outs),
        compiler_params=pltpu.CompilerParams(vmem_limit_bytes=40 * 1024 * 1024),
        cost_estimate=pl.CostEstimate(flops=flops, bytes_accessed=moved, transcendentals=0),
    )(*operands)


def dot(a, b):
    return jnp.dot(a, b, preferred_element_type=jnp.float32)


def dot_t(a, b):
    return lax.dot_general(a, b, (((1,), (1,)), ((), ())), preferred_element_type=jnp.float32)


def pack_body(zl_ref, mine_ref, other_ref, order_ref, out_ref):
    third = out_ref.shape[1] // 3
    zl = zl_ref[0]
    for p in range(3):
        k = lax.rem(p - zl + 3, 3)
        cols = pl.ds(pl.multiple_of(k * third, third), third)
        rounded = (mine_ref[:, cols] + other_ref[:, cols]).astype(jnp.bfloat16)
        out_ref[:, p * third : (p + 1) * third] = dot(order_ref[...], rounded).astype(jnp.bfloat16)


def unpack_body(arrived_ref, place_ref, cos_ref, sin_ref, q_ref, kv_ref):
    rows = arrived_ref.shape[0]
    hd = cos_ref.shape[1]
    placed = dot(place_ref[...], arrived_ref[...])
    cosine, sine = cos_ref[...], sin_ref[...]

    def rope(h):
        x = placed[:, h * hd : (h + 1) * hd]
        return (x * cosine + pltpu.roll(x, hd // 2, 1) * sine).astype(jnp.bfloat16)

    for h in range(QH):
        q_ref[h * rows : (h + 1) * rows, :] = rope(h)
    kv_ref[:, :hd] = rope(QH)
    kv_ref[:, hd:] = placed[:, (QH + 1) * hd :].astype(jnp.bfloat16)


def attend_body(parts, first, last, stride, *refs):
    base_ref, start_ref, q_ref = refs[:3]
    kv_refs = refs[3 : 3 + parts]
    at = 3 + parts
    if not first:
        m_in, l_in, acc_in = refs[at : at + 3]
        at += 3
    if last:
        back_ref, out_ref = refs[at : at + 2]
    else:
        m_out, l_out, acc_out = refs[at : at + 3]
    rows = start_ref.shape[0]
    hd = q_ref.shape[1]
    scale = math.log2(math.e) / math.sqrt(hd)
    start = start_ref[...]
    query = base_ref[parts] * rows + lax.broadcasted_iota(jnp.int32, (rows, 1), 0)
    allowed = []
    for i, kv_ref in enumerate(kv_refs):
        n = kv_ref.shape[0]
        col = lax.broadcasted_iota(jnp.int32, (1, n), 1)
        key = base_ref[i] * rows + (col % rows) - (col // rows) * (stride * rows)
        allowed.append((key >= start) & (key <= query))
    done = []
    for h in range(QH):
        at_rows = slice(h * rows, (h + 1) * rows)
        q = q_ref[at_rows, :]
        scores = [
            jnp.where(ok, dot_t(q, kv_ref[:, :hd]), -jnp.inf) for ok, kv_ref in zip(allowed, kv_refs)
        ]
        largest = functools.reduce(
            jnp.maximum, [jnp.max(s, axis=1, keepdims=True) for s in scores]
        )
        if not first:
            m_old = m_in[at_rows, :][:, :1]
            largest = jnp.maximum(largest, m_old)
        total, acc = 0.0, 0.0
        for s, kv_ref in zip(scores, kv_refs):
            p = jnp.exp2((s - largest) * scale)
            total = total + jnp.sum(p, axis=1, keepdims=True)
            acc = acc + dot(p.astype(jnp.bfloat16), kv_ref[:, hd:])
        if not first:
            shrink = jnp.exp2((m_old - largest) * scale)
            total = total + l_in[at_rows, :][:, :1] * shrink
            acc = acc + acc_in[at_rows, :] * shrink
        if last:
            done.append((acc / total).astype(jnp.bfloat16))
        else:
            m_out[at_rows, :] = jnp.broadcast_to(largest, (rows, hd))
            l_out[at_rows, :] = jnp.broadcast_to(total, (rows, hd))
            acc_out[at_rows, :] = acc
    if last:
        for h in range(QH):
            out_ref[:, h * hd : (h + 1) * hd] = dot(back_ref[...], done[h]).astype(jnp.bfloat16)


def attend(queries, start, kv_parts, bases, own, stride, state=None, back=None):
    total, hd = queries.shape
    rows = total // QH
    scalars = jnp.stack([*bases, own]).astype(jnp.int32)
    operands = [scalars, start, queries, *kv_parts]
    if state is not None:
        operands += list(state)
    if back is not None:
        operands.append(back)
        outs = [jax.ShapeDtypeStruct((rows, total // rows * hd), jnp.bfloat16)]
    else:
        outs = [jax.ShapeDtypeStruct((total, hd), jnp.float32)] * 3
    keys = sum(part.shape[0] for part in kv_parts)
    body = functools.partial(
        attend_body, len(kv_parts), state is None, back is not None, stride
    )
    return kernel_call(body, outs, 1, 16 * total * keys * hd, operands)


def project_halves(normed, proj):
    rows, width = normed.shape
    core = lax.axis_index("core")
    half = width // 2
    shard = lax.dynamic_slice_in_dim(proj, core * half, half, 1)
    gathered = spread(shard, "y").reshape(-1, half)
    mine = lax.dynamic_slice_in_dim(normed, core * half, half, 1)
    theirs = swap_core(lax.dynamic_slice_in_dim(normed, (1 - core) * half, half, 1))
    gathered, mine, theirs = lax.optimization_barrier((gathered, mine, theirs))
    both = jnp.concatenate([mine, theirs], axis=0)
    cut = (half // 128 * 7 // 16) * 128
    two = spread(gathered[:, cut:], "x").reshape(-1, half - cut)
    one = gathered[:, :cut]
    one = jnp.stack([one, z_shift(one, -1), z_shift(one, 1)])
    two_before, two_after = z_shift(two, 1), z_shift(two, -1)
    one = spread(one, "x").transpose(1, 0, 2, 3).reshape(-1, cut)
    sum_one = dot_t(both[:, :cut], one)
    rest = both[:, cut:]
    sum_two = jnp.concatenate(
        [dot_t(rest, two), dot_t(rest, two_after), dot_t(rest, two_before)], axis=1
    )
    total = sum_one + sum_two
    return total[:rows], swap_core(total[rows:])


def one_hot_rows(target, count):
    return (target[None, :] == jnp.arange(count, dtype=jnp.int32)[:, None]).astype(jnp.bfloat16)


def per_device(hidden, norm_gain, proj, assign, lengths):
    row_count = hidden.shape[0]
    groups = lax.axis_size(DP)
    per_peer = row_count // groups
    my_group = lax.axis_index(DP)
    mine, other = project_halves(rms_normed(hidden, norm_gain), proj)
    column = assign[0]
    group_of = (column // row_count).reshape(groups, row_count)
    slot_of = (column % row_count).reshape(groups, row_count)
    row_ids = jnp.arange(row_count, dtype=jnp.int32)
    own_group = lax.dynamic_index_in_dim(group_of, my_group, 0, keepdims=False)
    same = (own_group[:, None] == own_group[None, :]) & (row_ids[None, :] < row_ids[:, None])
    own_slots = own_group * per_peer + jnp.sum(same.astype(jnp.int32), axis=1)
    to_me = group_of == my_group
    earlier = to_me[:, None, :] & (row_ids[None, None, :] < row_ids[None, :, None])
    rank = jnp.sum(earlier.astype(jnp.int32), axis=2)
    ranks = jnp.arange(per_peer, dtype=jnp.int32)
    hit = to_me[:, None, :] & (rank[:, None, :] == ranks[None, :, None])
    slot_at = jnp.sum(jnp.where(hit, slot_of[:, None, :], 0), axis=2).reshape(row_count)
    send_order = one_hot_rows(own_slots, row_count)
    place_order = one_hot_rows(slot_at, row_count)

    stream_id = lax.axis_index(FSDP)
    stream = stream_id * row_count + row_ids
    _, positions, starts = segment_info(stream, lengths[0])
    width = mine.shape[1]
    head_dim = width // (QH + 2)
    cosine, sine = rope_tables(positions, head_dim)

    zl = lax.axis_index("zl")
    bf16 = jnp.bfloat16
    outgoing = kernel_call(
        pack_body,
        [jax.ShapeDtypeStruct((row_count, width), bf16)],
        1,
        2 * row_count * row_count * width,
        [zl[None].astype(jnp.int32), mine, other, send_order],
    )[0]
    arrived = lax.all_to_all(
        outgoing.reshape(groups, per_peer, width), DP, split_axis=0, concat_axis=0, tiled=True
    ).reshape(row_count, width)
    queries, keypair = kernel_call(
        unpack_body,
        [
            jax.ShapeDtypeStruct((QH * row_count, head_dim), bf16),
            jax.ShapeDtypeStruct((row_count, 2 * head_dim), bf16),
        ],
        0,
        2 * row_count * row_count * width,
        [arrived, place_order, cosine, sine],
    )

    ring = SIZES["y"]
    peers = lax.axis_size(FSDP)
    depth = peers // 2 // ring
    blocks = [keypair]
    for j in range(1, depth + 1):
        pairs = [(i, i + j * ring) for i in range(peers - j * ring)]
        blocks.append(lax.ppermute(keypair, FSDP, pairs))
    column_blocks = jnp.concatenate(blocks, axis=0)
    start = starts[:, None]
    state = attend(queries, start, [column_blocks], [stream_id], stream_id, ring)
    y = lax.axis_index("y")
    forward, backward = column_blocks[: depth * row_count], column_blocks
    step_up = [(i, i + 1) for i in range(peers - 1)]
    step_down = [(i, (i - 1) % ring) for i in range(ring)]
    for step in range(1, ring // 2 + 1):
        forward = lax.ppermute(forward, FSDP, step_up)
        parts, bases = [forward], [stream_id - step]
        if step < ring // 2:
            backward = lax.ppermute(backward, "y", step_down)
            parts.append(backward)
            bases.append(stream_id - y + lax.rem(y + step, ring))
            state = attend(queries, start, parts, bases, stream_id, ring, state)
        else:
            outgoing_back = attend(
                queries, start, parts, bases, stream_id, ring, state, place_order.T
            )[0]
    returned = lax.all_to_all(
        outgoing_back.reshape(groups, per_peer, -1), DP, split_axis=0, concat_axis=0, tiled=True
    ).reshape(row_count, -1)
    return lax.dot_general(
        send_order, returned, (((0,), (0,)), ((), ())), preferred_element_type=jnp.float32
    ).astype(bf16)


def solution(mesh):
    shape = [SIZES[name] for name in FSDP + DP]
    fine = Mesh(mesh.devices.reshape(shape), FSDP + DP)
    in_specs = (P(FSDP + DP, None), P(), P(FSDP, None), P(FSDP, None), P(DP, None))
    return jax.shard_map(
        per_device, mesh=fine, in_specs=in_specs, out_specs=P(FSDP + DP, None), check_vma=False
    )
```
